32 devices in a mesh: dp: 4 (over y, x), tensor: 8 (over z, core).
Axes of the slice: x: 2, y: 2, z: 4, core: 2. Of those that a mesh axis runs over, the one named last changes fastest.
Arguments:
- hidden: bfloat16 [16384, 2048], P(('dp', 'tensor')), may hold values from -160 to 160
- gain: float32 [2048], replicated, may hold values from 0.5 to 1.5
- bias: float32 [2048], replicated, may hold values from -3 to 3
- embedding: bfloat16 [49152, 2048], P('tensor'), may hold values from -8 to 8
- targets: int32 [16384], P('dp'), may hold values from 0 to 49151
- lengths: int32 [16], replicated, may hold values from 1 to 1024, 10240 in all
- owner: int32 [16], replicated, may hold values from 0 to 15, each once
Outputs:
- log_prob: float32 [16384], P(('dp', 'tensor'))
- entropy: float32 [16384], P(('dp', 'tensor'))
The draws below stay inside these ranges and needn't reach their ends.
Inputs may be any that keep to these rules, and one draw needn't show every extreme that they name: `lengths`: each sequence's length is at most 1024, one is exactly 1024, and they sum to 10240. `owner`: a permutation of the sequences.
All inputs are finite; a program needn't handle non-finite values.
Results may differ from the reference program's by a relative error of at most 0.0036.
Values may be sent and summed in bfloat16 or wider, within the bound.
No kernel may reach another device: no remote copies, remote signals or barrier semaphores. Data moves between devices by JAX's collectives and lax.ppermute only.
A program may use at most 192 MiB of HBM per device.

```python
import math
import jax
import jax.numpy as jnp
import numpy as np
from jax import lax

D = 2048
V = 49152
SLOT = 1024
SEQS = 16
TOKENS = 16384


def make_table(key):
    base = jax.random.normal(jax.random.fold_in(key, 11), (V, D), jnp.float32)
    base = jnp.clip(base, -5.0, 5.0) * (3.0 / math.sqrt(D))
    index = jnp.arange(V, dtype=jnp.int32)
    stride = V // 16
    level = (index // stride).astype(jnp.float32)
    within = index % stride
    wanted_factor = jnp.maximum(1.6 + 0.1 * level, (110.0 + 10.0 * level) * math.sqrt(D) / (3.0 * D))
    scaled = base * jnp.where(within == 0, wanted_factor, 1.0)[:, None]
    noise = jax.random.normal(jax.random.fold_in(key, 12), (V, D), jnp.float32) * (0.5 / D)
    paired = jnp.roll(scaled, 1, axis=0) * 0.992 + noise
    return jnp.clip(jnp.where((within == 1)[:, None], paired, scaled), -8.0, 8.0)


def draw_embedding(key, part):
    return make_table(key).astype(jnp.bfloat16)


def draw_hidden(key, part):
    row_scale = jnp.exp(jax.random.uniform(jax.random.fold_in(key, 22), (TOKENS, 1), jnp.float32) * math.log(10.0))
    base = jnp.clip(jax.random.normal(jax.random.fold_in(key, 21), (TOKENS, D), jnp.float32), -5.0, 5.0)
    states = base * row_scale
    table = make_table(key)
    index = jnp.arange(TOKENS, dtype=jnp.int32)
    level = index // 61 % 16
    chosen = table[level * (V // 16)]
    states = jnp.where((index % 61 == 7)[:, None], chosen * 15.0 + base * 0.02, states)
    return jnp.clip(states, -160.0, 160.0).astype(jnp.bfloat16)


def with_ends(result, own_key, low, high):
    longest = result.shape.index(max(result.shape))
    spots = []
    for shift in (0, 1):
        where = [jax.random.randint(jax.random.fold_in(own_key, axis), (), 0, length) for axis, length in enumerate(result.shape)]
        where[longest] = (where[longest] + shift) % result.shape[longest]
        spots.append(tuple(where))
    return result.at[spots[0]].set(low).at[spots[1]].set(high)


def profile(number_of, total, most, slope):
    loads = [(1 << 20) // math.isqrt(standing ** slope) + 1 for standing in range(2, number_of + 1)]
    surplus, holding = total - most - (number_of - 1), [1] * (number_of - 1)
    while surplus > 0:
        free = [i for i in range(number_of - 1) if holding[i] < most]
        mass, remaining = sum([loads[i] for i in free]), surplus
        for i in free:
            addition = min(most - holding[i], max(1, remaining * loads[i] // mass), surplus)
            holding[i] = holding[i] + addition
            surplus = surplus - addition
    return np.array([most] + holding)


def ragged(rng, number_of, total, limit, lean):
    if number_of == 2:
        one = jax.random.randint(rng, (), max(1, total - limit), min(limit, total - 1) + 1)
        return jnp.stack([one, total - one])
    sizes = jnp.asarray(profile(number_of, total, limit, lean), jnp.int32)
    couples = (number_of - 1) // 2
    donor, receiver = sizes[1:1 + 2 * couples:2], sizes[2:2 + 2 * couples:2]
    margin = jnp.minimum(donor - 1, limit - receiver)
    shifted = jax.random.randint(jax.random.fold_in(rng, 1), (couples,), 0, 1 << 20) % (margin + 1)
    sizes = sizes.at[1:1 + 2 * couples:2].set(donor - shifted).at[2:2 + 2 * couples:2].set(receiver + shifted)
    return sizes[jax.random.permutation(jax.random.fold_in(rng, 2), number_of)]


def scatter_about(key, dims, scale, limit, kind=jnp.bfloat16):
    return jnp.clip(scale * jax.random.normal(key, dims, jnp.float32), -limit, limit).astype(kind)


def setup_inputs(seed: int = 0) -> dict:
    arg_keys = jax.random.split(jax.random.key(seed), 8)
    return {
        "hidden": draw_hidden(jax.random.fold_in(arg_keys[7], 71), 0),
        "gain": jnp.clip(1.0 + 0.1 * jax.random.normal(arg_keys[1], (D,), jnp.float32), 0.5, 1.5),
        "bias": scatter_about(arg_keys[2], (D,), 0.5, 3.0, jnp.float32),
        "embedding": draw_embedding(jax.random.fold_in(arg_keys[7], 71), 0),
        "targets": with_ends(jax.random.randint(arg_keys[4], (TOKENS,), 0, V), jax.random.fold_in(arg_keys[4], 1), 0, V - 1).astype(jnp.int32),
        "lengths": ragged(arg_keys[5], SEQS, SEQS * SLOT * 5 // 8, SLOT, 2).astype(jnp.int32),
        "owner": jax.random.permutation(arg_keys[6], SEQS).astype(jnp.int32),
    }


EPS = 1e-05

def layer_norm(states, gain, bias):
    values = states.astype(jnp.float32)
    center = values - lax.optimization_barrier(jnp.mean(values, axis=-1, keepdims=True))
    spread = lax.optimization_barrier(jnp.mean(center * center, axis=-1, keepdims=True))
    return (center * lax.rsqrt(spread + EPS) * gain + bias).astype(jnp.bfloat16)

def row_scores(normed, table, wanted):
    logits = jnp.dot(normed, table.T, preferred_element_type=jnp.float32)
    top = lax.optimization_barrier(jnp.max(logits, axis=1))
    weights = jnp.exp(logits - top[:, None])
    total = lax.optimization_barrier(jnp.sum(weights, axis=1))
    moment = lax.optimization_barrier(jnp.sum(weights * logits, axis=1))
    picked = jnp.take_along_axis(logits, wanted[:, None].astype(jnp.int32), axis=1)[:, 0]
    logz = top + jnp.log(total)
    return (picked - logz, logz - moment / total)

def reference(hidden, gain, bias, embedding, targets, lengths, owner):
    block = min(512, TOKENS)
    normed = layer_norm(hidden, gain, bias)

    def one_block(pair):
        return row_scores(pair[0], embedding, pair[1])
    token_lp, token_ent = lax.map(one_block, (normed.reshape(TOKENS // block, block, D), targets.reshape(TOKENS // block, block)))
    token_lp = token_lp.reshape(SEQS, SLOT)
    token_ent = token_ent.reshape(SEQS, SLOT)
    valid = jnp.arange(SLOT, dtype=jnp.int32)[None, :] < lengths[:, None]
    token_lp = jnp.where(valid, token_lp, 0.0)
    token_ent = jnp.where(valid, token_ent, 0.0)
    log_prob = jnp.zeros((SEQS, SLOT), jnp.float32).at[owner].set(token_lp).reshape(TOKENS)
    entropy = jnp.zeros((SEQS, SLOT), jnp.float32).at[owner].set(token_ent).reshape(TOKENS)
    return (log_prob, entropy)
```

```python
import functools
import math

import jax
import jax.numpy as jnp
from jax import lax
from jax.experimental import pallas as pl
from jax.experimental.pallas import tpu as pltpu
from jax.sharding import PartitionSpec as P

SLOT = 1024
BLOCK = 128
GROUP = 2 * BLOCK
EPS = 1e-05
LOG2E = 1.4426950408889634
LN2 = 0.6931471805599453
LOWEST = -1e30


def layer_norm(states, gain, bias):
    values = states.astype(jnp.float32)
    center = values - jnp.mean(values, axis=-1, keepdims=True)
    spread = jnp.mean(center * center, axis=-1, keepdims=True)
    return (center * lax.rsqrt(spread + EPS) * gain + bias).astype(jnp.bfloat16)


def score_kernel(chunk, blocks, sub, live_ref, start_ref, rows_ref, t_ref, e_ref, o_ref, x_ref, state, order, sems):
    step, steps = pl.program_id(0), pl.num_programs(0)
    tile = e_ref.shape[0]

    def copy(j, place):
        return pltpu.make_async_copy(
            rows_ref.at[pl.ds(j * BLOCK, BLOCK)], x_ref.at[pl.ds(pl.multiple_of(place * BLOCK, BLOCK), BLOCK)], sems.at[j]
        )

    @pl.when(step == 0)
    def _():
        state[:, 0] = jnp.full((blocks // 2, 8, GROUP), LOWEST, jnp.float32)
        state[:, 1:4] = jnp.zeros((blocks // 2, 3, 8, GROUP), jnp.float32)
        o_ref[...] = jnp.zeros_like(o_ref)
        count = jnp.int32(0)
        for j in range(blocks):
            alive = live_ref[chunk, j] > 0

            @pl.when(alive)
            def _():
                order[count] = j
                copy(j, count).start()

            count = count + alive.astype(jnp.int32)
        order[blocks] = count

        @pl.when(count < blocks)
        def _():
            order[count] = blocks

        place = jnp.int32(0)
        for j in range(blocks):
            alive = live_ref[chunk, j] > 0
            pl.when(alive)(copy(j, place).wait)
            place = place + alive.astype(jnp.int32)

    for g in range(blocks // 2):

        @pl.when(2 * g < order[blocks])
        def _():
            x = x_ref[g * GROUP : (g + 1) * GROUP, :]
            first, second = order[2 * g], order[2 * g + 1]
            wanted = jnp.concatenate([t_ref[first], t_ref[second]], axis=1)
            wanted = wanted - start_ref[0] - step * tile - lax.broadcasted_iota(jnp.int32, (8, GROUP), 0)
            top, total, moment, picked = (state[g, i] for i in range(4))
            for s in range(0, tile, sub):
                logits = lax.dot_general(
                    e_ref[s : s + sub, :], x, (((1,), (1,)), ((), ())), preferred_element_type=jnp.float32
                )
                logits = logits.reshape(sub // 8, 8, GROUP) * LOG2E
                index = lax.broadcasted_iota(jnp.int32, (sub // 8, 8, GROUP), 0) * 8 + s
                new = jnp.maximum(top, jnp.max(logits, axis=0))
                lower = top - new
                factor = jnp.exp2(lower)
                delta = logits - new[None]
                weights = jnp.exp2(delta)
                moment = factor * (moment + total * lower) + jnp.sum(weights * delta, axis=0)
                total = factor * total + jnp.sum(weights, axis=0)
                picked = picked + jnp.sum(jnp.where(wanted[None] == index, logits, 0.0), axis=0)
                top = new
            for i, value in enumerate((top, total, moment, picked)):
                state[g, i] = value

            @pl.when(step == steps - 1)
            def _():
                highest = jnp.max(top, axis=0, keepdims=True)
                lower = top - highest
                factor = jnp.exp2(lower)
                result = jnp.concatenate(
                    [
                        highest,
                        jnp.sum(total * factor, axis=0, keepdims=True),
                        jnp.sum((moment + total * lower) * factor, axis=0, keepdims=True),
                        jnp.sum(picked, axis=0, keepdims=True),
                    ],
                    axis=0,
                )
                o_ref[first, 0:4] = result[:, 0:BLOCK]
                o_ref[second, 0:4] = result[:, BLOCK:GROUP]


def score(chunk, rows, table, targets, live, start):
    blocks, (vocab, width) = rows.shape[0] // BLOCK, table.shape
    tile = math.gcd(vocab, 768)
    sub = math.gcd(tile, 256)
    hbm = lambda a: pltpu.with_memory_space_constraint(a, pltpu.HBM)
    return pl.pallas_call(
        functools.partial(score_kernel, chunk, blocks, sub),
        out_shape=jax.ShapeDtypeStruct((blocks + 1, 8, BLOCK), jnp.float32),
        grid_spec=pltpu.PrefetchScalarGridSpec(
            num_scalar_prefetch=2,
            grid=(vocab // tile,),
            in_specs=[
                pl.BlockSpec(memory_space=pl.ANY),
                pl.BlockSpec((blocks + 1, 1, BLOCK), lambda i, *_: (0, 0, 0)),
                pl.BlockSpec((tile, width), lambda i, *_: (i, 0)),
            ],
            out_specs=pl.BlockSpec((blocks + 1, 8, BLOCK), lambda i, *_: (0, 0, 0)),
            scratch_shapes=[
                pltpu.VMEM((blocks * BLOCK, width), jnp.bfloat16),
                pltpu.VMEM((blocks // 2, 4, 8, GROUP), jnp.float32),
                pltpu.SMEM((blocks + 1,), jnp.int32),
                pltpu.SemaphoreType.DMA((blocks,)),
            ],
        ),
        compiler_params=pltpu.CompilerParams(vmem_limit_bytes=40 * 2**20),
        cost_estimate=pl.CostEstimate(
            flops=blocks * BLOCK * vocab * width * 2,
            bytes_accessed=vocab * width * 2,
            transcendentals=blocks * BLOCK * vocab,
        ),
    )(live, start, hbm(rows), targets, hbm(table))


def column_stats(normed, table, targets, lengths, start):
    rows, n_tensor = normed.shape[0], lax.axis_size("tensor")
    each = min(rows, BLOCK)
    chunks, blocks = rows // each, n_tensor * each // BLOCK
    stride = max(rows, BLOCK)
    first = jnp.arange(chunks)[:, None] * BLOCK + jnp.arange(blocks)[None, :] * stride
    live = jnp.clip(lengths[first // SLOT] - first % SLOT, 0, BLOCK).astype(jnp.int32)
    targets = targets.reshape(blocks, chunks, 1, BLOCK)
    spare = jnp.full((1, 1, BLOCK), -1, jnp.int32)
    done = []
    for c in range(chunks):
        gathered = lax.all_gather(normed[c * each : (c + 1) * each], "tensor", axis=0, tiled=True)
        wanted = jnp.concatenate([targets[:, c], spare], axis=0)
        done.append(score(c, gathered, table, wanted, live, start)[:blocks, :4])
    return jnp.stack(done, axis=1).reshape(blocks * chunks, 4, BLOCK)


def shards(hidden, gain, bias, embedding, targets, lengths, owner):
    rows = hidden.shape[0]
    n_dp, n_tensor = lax.axis_size("dp"), lax.axis_size("tensor")
    tp_index, dp_index = lax.axis_index("tensor"), lax.axis_index("dp")
    group = lengths.shape[0] // n_dp
    start = (tp_index * embedding.shape[0]).astype(jnp.int32)[None]
    own_lengths = lax.dynamic_slice_in_dim(lengths, dp_index * group, group)
    stats = column_stats(layer_norm(hidden, gain, bias), embedding, targets, own_lengths, start)
    parts = SLOT // rows
    stats = stats.reshape(group, SLOT // BLOCK, 4, BLOCK).transpose(0, 2, 1, 3).reshape(group, 4, parts, rows)
    stats = stats.transpose(0, 2, 1, 3)
    came_from = jnp.argsort(owner).astype(jnp.int32)
    local = came_from.reshape(n_dp, group) - dp_index * group
    outgoing = jnp.zeros((n_dp, group, parts, 4, rows), jnp.float32)
    for s in range(group):
        outgoing = jnp.where((local == s)[:, :, None, None, None], stats[s][None, None], outgoing)
    incoming = lax.all_to_all(
        outgoing.reshape(n_dp * n_tensor, 4, rows), ("dp", "tensor"), split_axis=0, concat_axis=0, tiled=True
    )
    place = dp_index * group + tp_index // parts
    sequence = lax.dynamic_slice_in_dim(came_from, place, 1)[0]
    incoming = incoming.reshape(n_dp, n_tensor, 4, rows)
    mine = lax.dynamic_slice_in_dim(incoming, sequence // group, 1, 0)[0]
    top = jnp.max(mine[:, 0], axis=0)
    lower = mine[:, 0] - top[None]
    factor = jnp.exp2(lower)
    total = jnp.sum(mine[:, 1] * factor, axis=0)
    moment = jnp.sum((mine[:, 2] + mine[:, 1] * lower) * factor, axis=0)
    picked = jnp.sum(mine[:, 3], axis=0)
    log_total = jnp.log(total)
    token_lp = (picked - top) * LN2 - log_total
    token_ent = log_total - moment * LN2 / total
    length = lax.dynamic_slice_in_dim(lengths, sequence, 1)[0]
    valid = jnp.arange(rows, dtype=jnp.int32) + tp_index % parts * rows < length
    return jnp.where(valid, token_lp, 0.0), jnp.where(valid, token_ent, 0.0)


def solution(mesh):
    in_specs = (P(("dp", "tensor"), None), P(), P(), P("tensor", None), P("dp"), P(), P())
    out_specs = (P(("dp", "tensor")), P(("dp", "tensor")))
    return jax.shard_map(shards, mesh=mesh, in_specs=in_specs, out_specs=out_specs, check_vma=False)
```

```python
import functools
import math

import jax
import jax.numpy as jnp
from jax import lax
from jax.experimental import pallas as pl
from jax.experimental.pallas import tpu as pltpu
from jax.sharding import PartitionSpec as P

SLOT = 1024
BLOCK = 128
WIDE = 4
EPS = 1e-05
LOG2E = 1.4426950408889634
LN2 = 0.6931471805599453
LOWEST = -1e30


def layer_norm(states, gain, bias):
    values = states.astype(jnp.float32)
    center = values - jnp.mean(values, axis=-1, keepdims=True)
    spread = jnp.mean(center * center, axis=-1, keepdims=True)
    return (center * lax.rsqrt(spread + EPS) * gain + bias).astype(jnp.bfloat16)


def score_kernel(call, sources, arrivals, shares, per, capacity, sub, lengths_ref, *refs):
    count = sum(arrival <= call for arrival in arrivals)
    rows_refs, (t_ref, e_ref), refs = refs[:count], refs[count : count + 2], refs[count + 2 :]
    stats_ref, (o_ref, x_ref, state, order, sems) = (None if call == 0 else refs[0]), refs[-5:]
    step, steps = pl.program_id(0), pl.num_programs(0)
    tile = e_ref.shape[0]
    spare = o_ref.shape[0] - 1
    slots = SLOT // BLOCK
    n_dp, n_tensor = lax.axis_size("dp"), lax.axis_size("tensor")
    group_size = lengths_ref.shape[0] // n_dp
    before = lax.axis_index("dp") * group_size
    start = lax.axis_index("tensor") * e_ref.shape[0] * steps
    chip, core = lax.axis_index("tensor") // 2, lax.axis_index("tensor") % 2

    def copy(ref, j, place):
        return pltpu.make_async_copy(
            ref.at[pl.ds(j * BLOCK, BLOCK)],
            x_ref.at[pl.ds(pl.multiple_of(place * BLOCK, BLOCK), BLOCK)],
            sems.at[place],
        )

    @pl.when(step == 0)
    def _():
        o_ref[...] = jnp.zeros_like(o_ref) if stats_ref is None else stats_ref[...]
        total = jnp.int32(0)
        for s in range(group_size):
            total = total + (lengths_ref[before + s] + BLOCK - 1) // BLOCK
        limits = [(total * share + 31) // 32 for share in shares]
        used, rank = jnp.int32(0), jnp.int32(0)
        for i in range(count):
            if sources is None:
                first, inside = jnp.int32(0), True
            else:
                away, crossed = sources[i]
                layer = chip + away * (2 * core - 1)
                half = core if not crossed else 1 - core
                inside = (layer >= 0) & (layer < n_tensor // 2)
                first = jnp.clip(layer, 0, n_tensor // 2 - 1) * slots + half * per
            for j in range(per):
                place = first + j
                live = inside & (lengths_ref[before + place // slots] > place % slots * BLOCK)
                mine = live
                if call > 0 and arrivals[i] < call:
                    mine = mine & (rank >= limits[call - 1])
                if call < len(shares):
                    mine = mine & (rank < limits[call])

                @pl.when(mine)
                def _():
                    order[used] = place
                    copy(rows_refs[i], j, used).start()

                used = used + mine.astype(jnp.int32)
                rank = rank + live.astype(jnp.int32)
        order[capacity + WIDE] = used
        for j in range(WIDE):
            order[used + j] = spare

    used = order[capacity + WIDE]

    def group(g, width):
        lanes = width * BLOCK
        begin = pl.multiple_of(g * (WIDE * BLOCK), WIDE * BLOCK)

        @pl.when(step == 0)
        def _():
            state[g, 0, :, 0:lanes] = jnp.full((8, lanes), LOWEST, jnp.float32)
            state[g, 1:4, :, 0:lanes] = jnp.zeros((3, 8, lanes), jnp.float32)
            for j in range(width):
                pl.when(g * WIDE + j < used)(copy(rows_refs[0], 0, g * WIDE + j).wait)

        x = x_ref[pl.ds(begin, lanes), :]
        places = [order[g * WIDE + j] for j in range(width)]
        wanted = jnp.concatenate([t_ref[jnp.minimum(p, spare - 1)] for p in places], axis=1)
        wanted = wanted - start - step * tile - lax.broadcasted_iota(jnp.int32, (8, lanes), 0)
        top, total, moment, picked = (state[g, i, :, 0:lanes] for i in range(4))
        for s in range(0, tile, sub):
            logits = lax.dot_general(
                e_ref[s : s + sub, :], x, (((1,), (1,)), ((), ())), preferred_element_type=jnp.float32
            )
            logits = logits.reshape(sub // 8, 8, lanes) * LOG2E
            index = lax.broadcasted_iota(jnp.int32, (sub // 8, 8, lanes), 0) * 8 + s
            new = jnp.maximum(top, jnp.max(logits, axis=0))
            lower = top - new
            factor = jnp.exp2(lower)
            delta = logits - new[None]
            weights = jnp.exp2(delta)
            moment = factor * (moment + total * lower) + jnp.sum(weights * delta, axis=0)
            total = factor * total + jnp.sum(weights, axis=0)
            picked = picked + jnp.sum(jnp.where(wanted[None] == index, logits, 0.0), axis=0)
            top = new
        for i, value in enumerate((top, total, moment, picked)):
            state[g, i, :, 0:lanes] = value

        @pl.when(step == steps - 1)
        def _():
            highest = jnp.max(top, axis=0, keepdims=True)
            lower = top - highest
            factor = jnp.exp2(lower)
            result = jnp.concatenate(
                [
                    highest,
                    jnp.sum(total * factor, axis=0, keepdims=True),
                    jnp.sum((moment + total * lower) * factor, axis=0, keepdims=True),
                    jnp.sum(picked, axis=0, keepdims=True),
                ],
                axis=0,
            )
            for j, p in enumerate(places):
                o_ref[p, 0:4] = result[:, j * BLOCK : (j + 1) * BLOCK]

    whole = (used + WIDE // 2 - 1) // WIDE

    def wide(g, carry):
        group(g, WIDE)
        return carry

    lax.fori_loop(0, whole, wide, 0)
    pl.when(whole * WIDE < used)(lambda: group(whole, WIDE // 2))


def score(call, pieces, sources, arrivals, shares, per, table, targets, lengths, stats):
    vocab, width = table.shape
    column = targets.shape[0]
    blocks = per * sum(arrival <= call for arrival in arrivals)
    capacity = -(-min(blocks, column) // WIDE) * WIDE
    tile = math.gcd(vocab, 768)
    sub = math.gcd(tile, 256)
    hbm = lambda a: pltpu.with_memory_space_constraint(a, pltpu.HBM)
    whole = lambda *shape: pl.BlockSpec(shape, lambda i, *_: (0, 0, 0))
    out = jax.ShapeDtypeStruct((column + 1, 8, BLOCK), jnp.float32)
    earlier = [] if call == 0 else [stats]
    return pl.pallas_call(
        functools.partial(score_kernel, call, sources, arrivals, shares, per, capacity, sub),
        out_shape=out,
        grid_spec=pltpu.PrefetchScalarGridSpec(
            num_scalar_prefetch=1,
            grid=(vocab // tile,),
            in_specs=[pl.BlockSpec(memory_space=pl.ANY)] * len(pieces)
            + [whole(*targets.shape), pl.BlockSpec((tile, width), lambda i, *_: (i, 0))]
            + [whole(*out.shape)] * len(earlier),
            out_specs=whole(*out.shape),
            scratch_shapes=[
                pltpu.VMEM((capacity * BLOCK, width), jnp.bfloat16),
                pltpu.VMEM((capacity // WIDE, 4, 8, WIDE * BLOCK), jnp.float32),
                pltpu.SMEM((capacity + WIDE + 1,), jnp.int32),
                pltpu.SemaphoreType.DMA((capacity,)),
            ],
        ),
        compiler_params=pltpu.CompilerParams(vmem_limit_bytes=40 * 2**20),
        cost_estimate=pl.CostEstimate(flops=2**20, bytes_accessed=2**10, transcendentals=0),
    )(lengths, *map(hbm, pieces), targets, hbm(table), *earlier)


def after(value, other):
    return lax.optimization_barrier((value, other))[0]


def finish(incoming):
    top = jnp.max(incoming[:, 0], axis=0)
    lower = incoming[:, 0] - top[None]
    factor = jnp.exp2(lower)
    total = jnp.sum(incoming[:, 1] * factor, axis=0)
    moment = jnp.sum((incoming[:, 2] + incoming[:, 1] * lower) * factor, axis=0)
    picked = jnp.sum(incoming[:, 3], axis=0)
    log_total = jnp.log(total)
    return (picked - top) * LN2 - log_total, log_total - moment * LN2 / total


def masked(results, lengths, sequence, first):
    length = lax.dynamic_slice_in_dim(lengths, sequence, 1)[0]
    valid = jnp.arange(results[0].shape[0], dtype=jnp.int32) + first < length
    return tuple(jnp.where(valid, result, 0.0) for result in results)


def column_stats(normed, table, targets, lengths):
    rows, n_tensor = normed.shape[0], lax.axis_size("tensor")
    column = rows * n_tensor // BLOCK
    targets = targets.reshape(column, 1, BLOCK)
    if 2 * rows != SLOT or n_tensor != 8:
        gathered = lax.all_gather(normed, "tensor", axis=0, tiled=True)
        return score(0, [gathered], None, [0], [], column, table, targets, lengths, None)[:column, :4]

    chips = n_tensor // 2
    swap = [(t, t ^ 1) for t in range(n_tensor)]
    along = [(2 * c, 2 * c + 2) for c in range(chips - 1)] + [(2 * c + 3, 2 * c + 1) for c in range(chips - 1)]
    along += [(n_tensor - 2, n_tensor - 1), (1, 0)]
    stages = [
        ([], [(1, 0), (1, 1)]),
        ([(1, 0), (1, 1)], [(2, 0), (2, 1)]),
        ([(2, 0), (2, 1)], [(3, 0), (3, 1)]),
        ([(3, 0)], []),
        ([(3, 1)], []),
    ]
    sources, arrivals = [(0, False), (0, True)], [0, 0]
    for stage, (arriving, _) in enumerate(stages):
        for hop, half in arriving:
            sources += [(hop, half == 1), (-hop, half == 0)]
            arrivals += [stage, stage]
    shares = [8, 16, 24, 28]

    moving = [normed, lax.ppermute(normed, "tensor", swap)]
    pieces, stats = list(moving), None
    for stage, (arriving, leaving) in enumerate(stages):
        for hop, half in arriving:
            moving[half] = after(moving[half], stats)
            pieces += [moving[half], lax.ppermute(moving[half], "tensor", swap)]
        for hop, half in leaving:
            moving[half] = lax.ppermute(moving[half], "tensor", along)
        stats = score(stage, pieces, sources, arrivals, shares, rows // BLOCK, table, targets, lengths, stats)
    return stats[:column, :4]


def shards(hidden, gain, bias, embedding, targets, lengths, owner):
    rows = hidden.shape[0]
    n_dp, n_tensor = lax.axis_size("dp"), lax.axis_size("tensor")
    tp_index, dp_index = lax.axis_index("tensor"), lax.axis_index("dp")
    group = lengths.shape[0] // n_dp
    stats = column_stats(layer_norm(hidden, gain, bias), embedding, targets, lengths)
    parts = SLOT // rows
    stats = stats.reshape(group, SLOT // BLOCK, 4, BLOCK).transpose(0, 2, 1, 3).reshape(group, 4, parts, rows)
    stats = stats.transpose(0, 2, 1, 3)
    came_from = jnp.argsort(owner).astype(jnp.int32)
    local = came_from.reshape(n_dp, group) - dp_index * group
    outgoing = jnp.zeros((n_dp, group, parts, 4, rows), jnp.float32)
    for s in range(group):
        outgoing = jnp.where((local == s)[:, :, None, None, None], stats[s][None, None], outgoing)
    incoming = lax.all_to_all(
        outgoing.reshape(n_dp * n_tensor, 4, rows), ("dp", "tensor"), split_axis=0, concat_axis=0, tiled=True
    )
    incoming = jnp.sum(incoming.reshape(n_dp, n_tensor, 4, rows), axis=0)
    sequence = lax.dynamic_slice_in_dim(came_from, dp_index * group + tp_index // parts, 1)[0]
    return masked(finish(incoming), lengths, sequence, tp_index % parts * rows)


def solution(mesh):
    in_specs = (P(("dp", "tensor"), None), P(), P(), P("tensor", None), P("dp"), P(), P())
    out_specs = (P(("dp", "tensor")), P(("dp", "tensor")))
    return jax.shard_map(shards, mesh=mesh, in_specs=in_specs, out_specs=out_specs, check_vma=False)
```

```python
import functools
import math

import jax
import jax.numpy as jnp
from jax import lax
from jax.experimental import pallas as pl
from jax.experimental.pallas import tpu as pltpu
from jax.sharding import PartitionSpec as P

SLOT = 1024
BLOCK = 128
WIDE = 4
ROOM = 30
EPS = 1e-05
LOG2E = 1.4426950408889634
LN2 = 0.6931471805599453
LOWEST = -1e30


def layer_norm(states, gain, bias):
    values = states.astype(jnp.float32)
    center = values - jnp.mean(values, axis=-1, keepdims=True)
    spread = jnp.mean(center * center, axis=-1, keepdims=True)
    return (center * lax.rsqrt(spread + EPS) * gain + bias).astype(jnp.bfloat16)


def score_kernel(call, sources, arrivals, limit, per, tile, sub, streamed, lengths_ref, *refs):
    count = sum(arrival <= call for arrival in arrivals)
    rows_refs, (t_ref, e_ref), refs = refs[:count], refs[count : count + 2], refs[count + 2 :]
    stats_ref, (o_ref, x_ref, state, order, sems) = (None if call == 0 else refs[0]), refs[-5:]
    at_tile, tiles = (pl.program_id(0), pl.num_programs(0)) if streamed else (0, e_ref.shape[0] // tile)
    once = pl.when(at_tile == 0) if streamed else lambda f: f()
    spare = o_ref.shape[0] - 1
    slots = SLOT // BLOCK
    n_dp, n_tensor = lax.axis_size("dp"), lax.axis_size("tensor")
    before = lax.axis_index("dp") * (lengths_ref.shape[0] // n_dp)
    start = lax.axis_index("tensor") * (tiles * tile)
    chip, core = lax.axis_index("tensor") // 2, lax.axis_index("tensor") % 2

    def copy(ref, j, place):
        return pltpu.make_async_copy(
            ref.at[pl.ds(j * BLOCK, BLOCK)],
            x_ref.at[pl.ds(pl.multiple_of(place * BLOCK, BLOCK), BLOCK)],
            sems.at[place],
        )

    def first_of(i):
        if sources is None:
            return jnp.int32(0), True
        away, crossed = sources[i]
        layer = chip + away * (2 * core - 1)
        half = core if not crossed else 1 - core
        inside = (layer >= 0) & (layer < n_tensor // 2)
        return jnp.clip(layer, 0, n_tensor // 2 - 1) * slots + half * per, inside

    @once
    def _():
        taken, arrived = jnp.int32(0), jnp.int32(0)
        for earlier in range(call):
            for i in range(count):
                if arrivals[i] == earlier:
                    first, inside = first_of(i)
                    length = lengths_ref[before + first // slots] - first % slots * BLOCK
                    held = jnp.clip((length + BLOCK - 1) // BLOCK, 0, per)
                    arrived = arrived + jnp.where(inside, held, 0)
            taken = jnp.minimum(taken + limit, arrived)
        used, rank = jnp.int32(0), jnp.int32(0)
        for i in range(count):
            first, inside = first_of(i)
            for j in range(per):
                place = first + j
                live = inside & (lengths_ref[before + place // slots] > place % slots * BLOCK)
                mine = live & (rank >= taken) & (rank < taken + limit)

                @pl.when(mine)
                def _():
                    order[used] = place
                    copy(rows_refs[i], j, used).start()

                used = used + mine.astype(jnp.int32)
                rank = rank + live.astype(jnp.int32)
        for j in range(WIDE):
            order[used + j] = spare
        order[limit + WIDE] = used
        o_ref[...] = jnp.zeros_like(o_ref) if stats_ref is None else stats_ref[...]

    used = order[limit + WIDE]

    def group(g, width):
        lanes = width * BLOCK
        begin = pl.multiple_of(g * (WIDE * BLOCK), WIDE * BLOCK)

        @once
        def _():
            for j in range(width):
                pl.when(g * WIDE + j < used)(copy(rows_refs[0], 0, g * WIDE + j).wait)
            state[g, 0, :, 0:lanes] = jnp.full((8, lanes), LOWEST, jnp.float32)
            state[g, 1:4, :, 0:lanes] = jnp.zeros((3, 8, lanes), jnp.float32)

        x = x_ref[pl.ds(begin, lanes), :]
        places = [order[g * WIDE + j] for j in range(width)]
        target = jnp.concatenate([t_ref[jnp.minimum(p, spare - 1)] for p in places], axis=1)
        target = target - start - lax.broadcasted_iota(jnp.int32, (8, lanes), 0)

        def step(i, carry, base=0):
            top, total, moment, picked = carry
            wanted = target - (base + i) * tile
            for s in range(0, tile, sub):
                table = e_ref[pl.ds(pl.multiple_of(i * tile + s, sub), sub), :]
                logits = lax.dot_general(table, x, (((1,), (1,)), ((), ())), preferred_element_type=jnp.float32)
                logits = logits.reshape(sub // 8, 8, lanes) * LOG2E
                new = jnp.maximum(top, jnp.max(logits, axis=0))
                lower = top - new
                factor = jnp.exp2(lower)
                delta = logits - new[None]
                weights = jnp.exp2(delta)
                moment = factor * (moment + total * lower) + jnp.sum(weights * delta, axis=0)
                total = factor * total + jnp.sum(weights, axis=0)
                for r in range(sub // 8):
                    picked = jnp.where(wanted == s + r * 8, logits[r], picked)
                top = new
            return top, total, moment, picked

        def give(top, total, moment, picked):
            highest = jnp.max(top, axis=0, keepdims=True)
            lower = top - highest
            factor = jnp.exp2(lower)
            result = jnp.concatenate(
                [
                    highest,
                    jnp.sum(total * factor, axis=0, keepdims=True),
                    jnp.sum((moment + total * lower) * factor, axis=0, keepdims=True),
                    jnp.sum(picked, axis=0, keepdims=True),
                ],
                axis=0,
            )
            for j, p in enumerate(places):
                o_ref[p, 0:4] = result[:, j * BLOCK : (j + 1) * BLOCK]

        carry = tuple(state[g, i, :, 0:lanes] for i in range(4))
        if streamed:
            carry = step(0, carry, at_tile)
            for i, value in enumerate(carry):
                state[g, i, :, 0:lanes] = value
            pl.when(at_tile == tiles - 1)(functools.partial(give, *carry))
        else:
            give(*lax.fori_loop(0, tiles, step, carry))

    whole = (used + WIDE // 2 - 1) // WIDE

    def wide(g, carry):
        group(g, WIDE)
        return carry

    lax.fori_loop(0, whole, wide, 0)
    pl.when(whole * WIDE < used)(lambda: group(whole, WIDE // 2))


def score(call, pieces, sources, arrivals, limit, per, table, targets, lengths, stats):
    vocab, width = table.shape
    column = targets.shape[0]
    streamed = call in (0, 4)
    tile = math.gcd(vocab, 768 if streamed else 1536)
    sub = math.gcd(tile, 256)
    space = pltpu.HBM if streamed else pltpu.VMEM
    hbm = lambda a: pltpu.with_memory_space_constraint(a, pltpu.HBM)
    vmem = pl.BlockSpec(memory_space=pltpu.VMEM)
    whole = lambda a: pl.BlockSpec(a.shape, lambda i: (0, 0, 0)) if streamed else vmem
    earlier = [] if call == 0 else [stats]
    out = jax.ShapeDtypeStruct((column + 1, 8, BLOCK), jnp.float32)
    return pl.pallas_call(
        functools.partial(score_kernel, call, sources, arrivals, limit, per, tile, sub, streamed),
        out_shape=out,
        grid=(vocab // tile,) if streamed else (),
        in_specs=[pl.BlockSpec(memory_space=pltpu.SMEM)]
        + [pl.BlockSpec(memory_space=pl.ANY)] * len(pieces)
        + [whole(targets), pl.BlockSpec((tile, width), lambda i: (i, 0)) if streamed else vmem]
        + [whole(out)] * len(earlier),
        out_specs=whole(out),
        scratch_shapes=[
            pltpu.VMEM((limit * BLOCK, width), jnp.bfloat16),
            pltpu.VMEM((-(-limit // WIDE), 4, 8, WIDE * BLOCK), jnp.float32),
            pltpu.SMEM((limit + WIDE + 1,), jnp.int32),
            pltpu.SemaphoreType.DMA((limit,)),
        ],
        compiler_params=pltpu.CompilerParams(vmem_limit_bytes=ROOM * 2**20 + max(limit - 8, 0) * BLOCK * width * 2),
        cost_estimate=pl.CostEstimate(flops=2**20, bytes_accessed=2**10, transcendentals=0),
    )(lengths, *map(hbm, pieces), targets, pltpu.with_memory_space_constraint(table, space), *earlier)


def after(value, other):
    return lax.optimization_barrier((value, other))[0]


def finish(incoming):
    top = jnp.max(incoming[:, 0], axis=0)
    lower = incoming[:, 0] - top[None]
    factor = jnp.exp2(lower)
    total = jnp.sum(incoming[:, 1] * factor, axis=0)
    moment = jnp.sum((incoming[:, 2] + incoming[:, 1] * lower) * factor, axis=0)
    picked = jnp.sum(incoming[:, 3], axis=0)
    log_total = jnp.log(total)
    return (picked - top) * LN2 - log_total, log_total - moment * LN2 / total


def masked(results, lengths, sequence, first):
    length = lax.dynamic_slice_in_dim(lengths, sequence, 1)[0]
    valid = jnp.arange(results[0].shape[0], dtype=jnp.int32) + first < length
    return tuple(jnp.where(valid, result, 0.0) for result in results)


def column_stats(normed, table, targets, lengths):
    rows, n_tensor = normed.shape[0], lax.axis_size("tensor")
    column = rows * n_tensor // BLOCK
    targets = targets.reshape(column, 1, BLOCK)
    if 2 * rows != SLOT or n_tensor != 8:
        gathered = lax.all_gather(normed, "tensor", axis=0, tiled=True)
        return score(0, [gathered], None, [0], column, column, table, targets, lengths, None)[:column, :4]

    chips = n_tensor // 2
    swap = [(t, t ^ 1) for t in range(n_tensor)]
    along = [(2 * c, 2 * c + 2) for c in range(chips - 1)] + [(2 * c + 3, 2 * c + 1) for c in range(chips - 1)]
    along += [(n_tensor - 2, n_tensor - 1), (1, 0)]
    stages = [
        ([], [(1, 0), (1, 1)]),
        ([(1, 0), (1, 1)], [(2, 0), (2, 1)]),
        ([(2, 0), (2, 1)], [(3, 0), (3, 1)]),
        ([(3, 0)], []),
        ([(3, 1)], []),
    ]
    sources, arrivals = [(0, False), (0, True)], [0, 0]
    for stage, (arriving, _) in enumerate(stages):
        for hop, half in arriving:
            sources += [(hop, half == 1), (-hop, half == 0)]
            arrivals += [stage, stage]
    per = rows // BLOCK

    moving = [normed, lax.ppermute(normed, "tensor", swap)]
    pieces, stats = list(moving), None
    for stage, (arriving, leaving) in enumerate(stages):
        for hop, half in arriving:
            moving[half] = after(moving[half], stats)
            pieces += [moving[half], lax.ppermute(moving[half], "tensor", swap)]
        for hop, half in leaving:
            moving[half] = lax.ppermute(moving[half], "tensor", along)
        stats = score(stage, pieces, sources, arrivals, 2 * per, per, table, targets, lengths, stats)
    return stats[:column, :4]


def shards(hidden, gain, bias, embedding, targets, lengths, owner):
    rows = hidden.shape[0]
    n_dp, n_tensor = lax.axis_size("dp"), lax.axis_size("tensor")
    tp_index, dp_index = lax.axis_index("tensor"), lax.axis_index("dp")
    group = lengths.shape[0] // n_dp
    stats = column_stats(layer_norm(hidden, gain, bias), embedding, targets, lengths)
    parts = SLOT // rows
    stats = stats.reshape(group, SLOT // BLOCK, 4, BLOCK).transpose(0, 2, 1, 3).reshape(group, 4, parts, rows)
    stats = stats.transpose(0, 2, 1, 3)
    index = jnp.arange(owner.shape[0], dtype=jnp.int32)
    came_from = jnp.sum(jnp.where(owner[None, :] == index[:, None], index[None, :], 0), axis=1)
    local = came_from.reshape(n_dp, group) - dp_index * group
    outgoing = jnp.zeros((n_dp, group, parts, 4, rows), jnp.float32)
    for s in range(group):
        outgoing = jnp.where((local == s)[:, :, None, None, None], stats[s][None, None], outgoing)
    incoming = lax.all_to_all(
        outgoing.reshape(n_dp * n_tensor, 4, rows), ("dp", "tensor"), split_axis=0, concat_axis=0, tiled=True
    )
    incoming = jnp.sum(incoming.reshape(n_dp, n_tensor, 4, rows), axis=0)
    sequence = lax.dynamic_slice_in_dim(came_from, dp_index * group + tp_index // parts, 1)[0]
    return masked(finish(incoming), lengths, sequence, tp_index % parts * rows)


def solution(mesh):
    in_specs = (P(("dp", "tensor"), None), P(), P(), P("tensor", None), P("dp"), P(), P())
    out_specs = (P(("dp", "tensor")), P(("dp", "tensor")))
    return jax.shard_map(shards, mesh=mesh, in_specs=in_specs, out_specs=out_specs, check_vma=False)
```
